32 devices in a mesh: dp: 2 (over core), expert: 16 (over z, y, x).
Axes of the slice: x: 2, y: 2, z: 4, core: 2. Of those that a mesh axis runs over, the one named last changes fastest.
Arguments:
- tokens: bfloat16 [2048, 2048], P(('dp', 'expert')), may hold values from -6 to 6
- tangent: bfloat16 [2048, 2048], P(('dp', 'expert'))
- adjoint: bfloat16 [2048, 2048], P(('dp', 'expert')), may hold values from -6 to 6
- gates: float32 [2048, 8], P(('dp', 'expert')), may hold values from 0.05 to 0.5
- expert_ids: int32 [2048, 8], P(('dp', 'expert')), may hold values from 0 to 31, all different within a row; in each aligned block of 64 rows (0 to 63, 64 to 127, ...) at most 32 rows name the same one
- w_gate: bfloat16 [32, 2048, 768], P('expert'), may hold values from -0.125 to 0.125
- w_up: bfloat16 [32, 2048, 768], P('expert'), may hold values from -0.125 to 0.125
- w_down: bfloat16 [32, 768, 2048], P('expert'), may hold values from -0.21875 to 0.21875
Outputs:
- hvp: float32 [2048, 2048], P(('dp', 'expert'))
- quotient: float32 [], replicated
The draws below stay inside these ranges and needn't reach their ends.
Inputs may be any that keep to these rules, and one draw needn't show every extreme that they name: `expert_ids`: each token names 8 different experts. Among the tokens of one device no expert is named more than 32 times, a bound that some block reaches; every expert is named somewhere.
All inputs are finite; a program needn't handle non-finite values.
Results may differ from the reference program's by a relative error of at most 0.0041.
Values may be sent and summed in bfloat16 or wider, within the bound.
No kernel may reach another device: no remote copies, remote signals or barrier semaphores. Data moves between devices by JAX's collectives and lax.ppermute only.
A program may use at most 128 MiB of HBM per device.

```python
import math
import jax
import jax.numpy as jnp
import numpy as np
from jax import lax

D = 2048
FF = 768
TOP = 8
TOK_DEV = 64
EXPERTS = 32
CAP = 32
TOKENS = 2048
N_DP = 2
N_EXPERT = 16


def draw_tangent(key, part):
    first_key = jax.random.fold_in(key, 0)
    rows = jnp.arange(TOKENS, dtype=jnp.float32)
    ramp = 1.0 + 2.0 * rows / (TOKENS - 1.0)
    base = jnp.clip(jax.random.normal(first_key, (TOKENS, D), jnp.float32), -6.0, 6.0)
    return (base * ramp[:, None]).astype(jnp.bfloat16)


def levels(own_key, dims, shards, low, largest):
    loudness, own = 1.0, jax.random.fold_in(own_key, 6)
    for dim, parts in shards:
        steps = jnp.exp(jax.random.uniform(jax.random.fold_in(own, dim), (parts,), jnp.float32, low / len(shards), largest / len(shards)))
        loudness = loudness * jnp.repeat(steps, dims[dim] // parts).reshape([-1 if axis == dim else 1 for axis in range(len(dims))])
    return loudness


def shared_out(rng, own, number, rows, count, top, bound, lean):
    order = jax.random.permutation(rng, count)
    crowded, common = portions_of(count, rows * top, bound, lean, True), portions_of(count, rows * top, bound, lean, False)
    places = jnp.arange(count)

    def named(tallies, turn):
        used = int((tallies > 0).sum())
        fixed = max(1, used // 4)
        moved = fixed + (places - fixed + turn * (used - fixed)) % max(1, count - fixed)
        return jnp.zeros((count,), jnp.int32).at[order[jnp.where(places < fixed, places, moved)]].set(jnp.asarray(tallies, jnp.int32))

    tallies = jnp.where(number % 4 == 0, named(crowded, number // 4), named(common, number - number // 4 - 1))
    mixed = jax.random.permutation(jax.random.fold_in(own, 3), count)
    donor, taker = mixed[0:count // 2 * 2:2], mixed[1:count // 2 * 2:2]
    slack = jnp.minimum(tallies[donor] - 1, bound - tallies[taker]) // 2
    slack = jnp.where((donor == order[0]) | (taker == order[0]) | (tallies[taker] == 0), 0, jnp.maximum(slack, 0))
    moved = jax.random.randint(jax.random.fold_in(own, 4), (count // 2,), 0, 1 << 20) % (slack + 1)
    tallies = tallies.at[donor].add(-moved).at[taker].add(moved)
    members = jnp.searchsorted(jnp.cumsum(tallies), jnp.arange(rows * top), side="right").astype(jnp.int32)
    listing = members.reshape(top, rows).T
    listing = listing[jax.random.permutation(jax.random.fold_in(own, 1), rows)]
    turn = jax.random.randint(jax.random.fold_in(own, 2), (rows, 1), 0, top)
    return jnp.take_along_axis(listing, (jnp.arange(top)[None, :] + turn) % top, axis=1)


def portions_of(count, total, reach, skew, full):
    weights = [(1 << 20) // math.isqrt(grade ** skew) + 1 for grade in range(1, count + 1)]
    largest = reach if full else min(reach, max(-(-total // count), total * weights[0] // sum(weights)))
    least = 1 if total - largest >= count - 1 else 0
    given, spare = [largest] + [least] * (count - 1), total - largest - least * (count - 1)
    while spare > 0:
        candidates = [i for i in range(1, count) if given[i] < largest] or [i for i in range(1, count) if given[i] < reach]
        pool, left = sum([weights[i] for i in candidates]), spare
        for i in candidates:
            addition = min(reach - given[i], max(1, left * weights[i] // pool), spare)
            given[i] = given[i] + addition
            spare = spare - addition
    return np.array(given)


def normal_values(key, extent, spread, bound, pieces=(), kind=jnp.bfloat16):
    array = spread * jax.random.normal(key, extent, jnp.float32)
    if pieces:
        array = array * levels(key, extent, pieces, -0.22, 0.18)
    return jnp.clip(array, -bound, bound).astype(kind)


def setup_inputs(seed: int = 0) -> dict:
    streams_of = jax.random.split(jax.random.key(seed), 9)
    tokens = normal_values(streams_of[0], (TOKENS, D), 1.0, 6.0, ((0, 32),))
    tangent = draw_tangent(jax.random.fold_in(streams_of[8], 71), 0)
    adjoint = normal_values(streams_of[2], (TOKENS, D), 1.0, 6.0, ((0, 32),))
    gates = jnp.clip(jnp.exp(math.log(0.5) - 2.3025851 * jax.random.uniform(streams_of[3], (TOKENS, TOP), jnp.float32) ** levels(streams_of[3], (TOKENS, TOP), ((0, 32),), -0.2, 0.2)), 0.05, 0.5)
    expert_ids_keys = jax.random.split(jax.random.fold_in(streams_of[4], 1), TOKENS // TOK_DEV)
    expert_ids_turns = jax.random.permutation(jax.random.fold_in(streams_of[4], 3), TOKENS // TOK_DEV)
    expert_ids = jax.vmap(lambda own, number: shared_out(jax.random.fold_in(streams_of[4], 2), own, number, TOK_DEV, EXPERTS, TOP, CAP, 2))(expert_ids_keys, expert_ids_turns).reshape((TOKENS, TOP))
    w_gate = normal_values(streams_of[5], (EXPERTS, D, FF), D ** -0.5, 0.125, ((0, 16),))
    w_up = normal_values(streams_of[6], (EXPERTS, D, FF), D ** -0.5, 0.125, ((0, 16),))
    w_down = normal_values(streams_of[7], (EXPERTS, FF, D), FF ** -0.5, 0.21875, ((0, 16),))
    return dict(tokens=tokens, tangent=tangent, adjoint=adjoint, gates=gates, expert_ids=expert_ids, w_gate=w_gate, w_up=w_up, w_down=w_down)


def expert_terms(primal_rows, tangent_rows, adjoint_rows, gate_mat, up_mat, down_mat):
    pre_gate = jnp.einsum("erd,edf->erf", primal_rows, gate_mat, preferred_element_type=jnp.float32)
    pre_up = jnp.einsum("erd,edf->erf", primal_rows, up_mat, preferred_element_type=jnp.float32)
    dir_gate = jnp.einsum("erd,edf->erf", tangent_rows, gate_mat, preferred_element_type=jnp.float32)
    dir_up = jnp.einsum("erd,edf->erf", tangent_rows, up_mat, preferred_element_type=jnp.float32)
    back_units = jnp.einsum("erd,efd->erf", adjoint_rows, down_mat, preferred_element_type=jnp.float32)
    sigmoid_g = jax.nn.sigmoid(pre_gate)
    first_der = sigmoid_g * (1.0 + pre_gate * (1.0 - sigmoid_g))
    second_der = sigmoid_g * (1.0 - sigmoid_g) * (2.0 + pre_gate * (1.0 - 2.0 * sigmoid_g))
    part_gate = (back_units * (dir_up * first_der + pre_up * second_der * dir_gate)).astype(jnp.bfloat16)
    part_up = (back_units * first_der * dir_gate).astype(jnp.bfloat16)
    result = jnp.einsum("erf,edf->erd", part_gate, gate_mat, preferred_element_type=jnp.float32)
    return result + jnp.einsum("erf,edf->erd", part_up, up_mat, preferred_element_type=jnp.float32)


def reference(tokens, tangent, adjoint, gates, expert_ids, w_gate, w_up, w_down):
    devices_all = N_DP * N_EXPERT
    tok_total, top_count = expert_ids.shape
    tok_rows = tok_total // devices_all
    width = tokens.shape[1]
    flat_ids = expert_ids.reshape(devices_all, tok_rows * top_count)
    onehot = (flat_ids[:, :, None] == jnp.arange(EXPERTS, dtype=jnp.int32)[None, None, :]).astype(jnp.int32)
    before = jnp.cumsum(onehot, axis=1) - onehot
    slot_index = jnp.sum(before * onehot, axis=2).astype(jnp.int32)
    device_index = jnp.arange(devices_all, dtype=jnp.int32)[:, None]
    per_expert = devices_all * CAP
    position = (flat_ids * per_expert + device_index * CAP + slot_index).reshape(-1).astype(jnp.int32)
    token_of = (jnp.arange(tok_total * top_count, dtype=jnp.int32) // top_count).astype(jnp.int32)
    owner = jnp.full((EXPERTS * per_expert,), tok_total, jnp.int32).at[position].set(token_of)
    zero_row = jnp.zeros((1, width), jnp.bfloat16)
    primal_pad = jnp.concatenate([tokens, zero_row], axis=0)
    tangent_pad = jnp.concatenate([tangent, zero_row], axis=0)
    adjoint_pad = jnp.concatenate([adjoint, zero_row], axis=0)

    def one_expert(packed):
        expert_index, gate_mat, up_mat, down_mat = packed
        picked = lax.dynamic_slice_in_dim(owner, (expert_index * per_expert).astype(jnp.int32), per_expert)
        terms = expert_terms(primal_pad[picked][None], tangent_pad[picked][None], adjoint_pad[picked][None],
                             gate_mat[None], up_mat[None], down_mat[None])[0]
        return terms.astype(jnp.bfloat16)

    replies = lax.map(one_expert, (jnp.arange(EXPERTS, dtype=jnp.int32), w_gate, w_up, w_down))
    replies = replies.reshape(EXPERTS * per_expert, width)
    picked_rows = replies[position].reshape(tok_total, top_count, width).astype(jnp.float32)
    hvp = jnp.sum(gates[:, :, None] * picked_rows, axis=1)
    tangent_wide = tangent.astype(jnp.float32)
    quotient = jnp.sum(hvp * hvp) / jnp.sum(tangent_wide * tangent_wide)
    return hvp, quotient
```

```python
import functools

import jax
import jax.numpy as jnp
from jax import lax
from jax.experimental import pallas as pl
from jax.experimental.pallas import tpu as pltpu
from jax.sharding import PartitionSpec as P

F32, BF16 = jnp.float32, jnp.bfloat16
NT = (((1,), (1,)), ((), ()))


def expert_kernel(shapes, part, start, *refs):
    count = len(shapes)
    pieces, (gates, w_gate, w_up, w_down) = refs[:count], refs[count : count + 4]
    outs, (both, adj, total) = refs[count + 4 : -3], refs[-3:]
    rows, width = adj.shape
    experts, _, hidden = w_gate.shape
    at = 0
    for piece, (blocks, r) in zip(pieces, shapes):
        for b in range(blocks):
            both[at : at + r] = piece[b, :r]
            both[rows + at : rows + at + r] = piece[b, r : 2 * r]
            adj[at : at + r] = piece[b, 2 * r :]
            at += r

    def parts_of(e, cols):
        gate = jnp.dot(both[...], w_gate[e, :, cols], preferred_element_type=F32)
        up = jnp.dot(both[...], w_up[e, :, cols], preferred_element_type=F32)
        back = lax.dot_general(w_down[e, cols, :], adj[...], NT, preferred_element_type=F32).T
        pre, pre_dir, lin, lin_dir = gate[:rows], gate[rows:], up[:rows], up[rows:]
        s = jax.nn.sigmoid(pre)
        first = s * (1.0 + pre * (1.0 - s))
        second = s * (1.0 - s) * (2.0 + pre * (1.0 - 2.0 * s))
        part_gate = back * (lin_dir * first + lin * second * pre_dir)
        part_up = back * first * pre_dir
        return part_gate.T.astype(BF16), part_up.T.astype(BF16)

    for e in range(experts):
        parts = [parts_of(e, slice(j, j + part)) for j in range(0, hidden, part)]
        part_gate = jnp.concatenate([p[0] for p in parts], axis=0)
        part_up = jnp.concatenate([p[1] for p in parts], axis=0)
        weight = gates[e, :, start : start + rows]
        chunk = 512 if width % 512 == 0 else width
        for c in range(0, width, chunk):
            cols = slice(c, c + chunk)
            reply = jnp.dot(w_gate[e, cols, :], part_gate, preferred_element_type=F32)
            reply += jnp.dot(w_up[e, cols, :], part_up, preferred_element_type=F32)
            term = jnp.where(weight != 0.0, weight * reply.astype(BF16).astype(F32), 0.0)
            if e > 0:
                term += total[cols, :]
            if e < experts - 1:
                total[cols, :] = term
                continue
            term = term.T
            at = 0
            for out in outs:
                blocks, r, _ = out.shape
                for b in range(blocks):
                    out[b, :, cols] = term[at : at + r].astype(out.dtype)
                    at += r


def expert_call(pieces, kinds, start, gates, w_gate, w_up, w_down):
    width = pieces[0].shape[2]
    shapes = tuple((p.shape[0], p.shape[1] // 3) for p in pieces)
    rows = sum(b * r for b, r in shapes)
    experts, _, hidden = w_gate.shape
    part = 256 if hidden % 256 == 0 else hidden
    near = pl.BlockSpec(memory_space=pltpu.VMEM)
    out_shape, at = [], 0
    for number, kind in kinds:
        group = shapes[at : at + number]
        out_shape.append(
            jax.ShapeDtypeStruct((sum(b for b, _ in group), group[0][1], width), kind)
        )
        at += number
    return pl.pallas_call(
        functools.partial(expert_kernel, shapes, part, start),
        in_specs=[near] * (len(pieces) + 4),
        out_specs=[near] * len(out_shape),
        out_shape=out_shape,
        scratch_shapes=[
            pltpu.VMEM((2 * rows, width), BF16),
            pltpu.VMEM((rows, width), BF16),
            pltpu.VMEM((width, rows), F32),
        ],
        compiler_params=pltpu.CompilerParams(vmem_limit_bytes=20 * 1024 * 1024),
        cost_estimate=pl.CostEstimate(
            flops=14 * rows * width * hidden * experts,
            bytes_accessed=8 * rows * width,
            transcendentals=rows * hidden * experts,
        ),
    )(*pieces, gates, w_gate, w_up, w_down)


def pack(ranges, *arrays):
    count, width = len(arrays), arrays[0].shape[1]

    def kernel(*refs):
        for out, (lo, hi) in zip(refs[count:], ranges):
            for i, ref in enumerate(refs[:count]):
                out[0, i * (hi - lo) : (i + 1) * (hi - lo)] = ref[lo:hi]

    near = pl.BlockSpec(memory_space=pltpu.VMEM)
    return pl.pallas_call(
        kernel,
        in_specs=[near] * count,
        out_specs=[near] * len(ranges),
        out_shape=[
            jax.ShapeDtypeStruct((1, count * (hi - lo), width), arrays[0].dtype)
            for lo, hi in ranges
        ],
        compiler_params=pltpu.CompilerParams(vmem_limit_bytes=4 * 1024 * 1024),
    )(*arrays)


def local(tokens, tangent, adjoint, gates, expert_ids, w_gate, w_up, w_down):
    count = lax.axis_size("expert")
    me = lax.axis_index("expert")
    ring = 4
    layer = count // ring
    high, low = me // layer, me % layer
    experts = w_gate.shape[0]
    tok_rows, _ = expert_ids.shape
    mats = (w_gate, w_up, w_down)

    def across(a, k):
        return lax.ppermute(a, "expert", [(i, i ^ k) for i in range(count)])

    def along(a, r):
        return lax.ppermute(a, "expert", [(i, (i + layer * r) % count) for i in range(count)])

    all_ids = jnp.arange(experts * count, dtype=jnp.int32)
    dense = jnp.sum(
        jnp.where(expert_ids[:, :, None] == all_ids[None, None, :], gates[:, :, None], 0.0), axis=1
    )
    dense = dense.T.reshape(count, experts, tok_rows)

    def to_owners(dense):
        return lax.all_to_all(dense, "expert", split_axis=0, concat_axis=0, tiled=True)

    def weights_of(dense, listing):
        source = ((high - jnp.arange(ring)) % ring * layer)[:, None] + (low ^ jnp.arange(layer))
        dense = jnp.take(dense, source.reshape(-1), axis=0).reshape(ring, layer, experts, tok_rows)
        parts = [dense[r, k, :, slice(*rows)] for blocks, k, rows in listing for r in blocks]
        return jnp.concatenate(parts, axis=1)[:, None, :]

    if layer == 4:
        arrays = (tokens, tangent, adjoint)
        hvp = scheduled(across, along, to_owners, weights_of, dense, arrays, mats)
    else:
        rows = (0, tok_rows)
        listing = [(range(ring), k, rows) for k in range(layer)]
        weights = weights_of(to_owners(dense), listing)
        blocks = list(pack([rows], tokens, tangent, adjoint))
        for _ in range(ring - 1):
            blocks.append(along(blocks[-1], 1))
        mine = jnp.concatenate(blocks, axis=0)
        column = 0.0
        for k in range(layer):
            piece = across(mine, k) if k else mine
            (reply,) = expert_call([piece], [(1, BF16)], k * ring * tok_rows, weights, *mats)
            column += (across(reply, k) if k else reply).astype(F32)
        hvp = column[0]
        for r in range(1, ring):
            hvp += along(column[r].astype(BF16), -r).astype(F32)

    wide = tangent.astype(F32)
    sums = jnp.stack([jnp.sum(hvp * hvp), jnp.sum(wide * wide)])
    ways = lax.axis_size("dp") * count
    sums = jnp.broadcast_to(sums[None, None, :], (ways, 1, 2))
    sums = lax.all_to_all(sums, ("dp", "expert"), split_axis=0, concat_axis=0, tiled=True)
    sums = jnp.sum(sums, axis=(0, 1))
    return hvp, sums[0] / sums[1]


def scheduled(across, along, to_owners, weights_of, dense, arrays, mats):
    bar = lambda *values: lax.optimization_barrier(values)
    join = lambda *values: jnp.concatenate(values, axis=0)
    f32 = lambda value: value.astype(F32)
    tok_rows = arrays[0].shape[0]
    rows_a, rows_b = (0, 3 * tok_rows // 4), (3 * tok_rows // 4, tok_rows)
    lo, hi, every = (0, 1), (2, 3), (0, 1, 2, 3)

    def spread(r):
        return [((r,), k, rows_b) for k in every]

    order = [
        [(lo, 1, rows_a), (lo, 2, rows_a)] + spread(0),
        [(hi, 1, rows_a), (hi, 2, rows_a)] + spread(1),
        [(lo, 0, rows_a), (hi, 0, rows_a)] + spread(2),
        [(lo, 3, rows_a), (hi, 3, rows_a)] + spread(3),
    ]
    sizes = [sum(len(b) * (rows[1] - rows[0]) for b, _, rows in part) for part in order]

    def call(place, pieces, kinds):
        return expert_call(pieces, kinds, sum(sizes[:place]), weights, *mats)

    own_a, own_b = pack([rows_a, rows_b], *arrays)
    z1 = along(own_a, 1)
    bx, by, bd = across(own_b, 1), across(own_b, 2), across(own_b, 3)
    dense = to_owners(dense)
    z1, bx, by, bd, own_a, own_b = bar(z1, bx, by, bd, own_a, own_b)
    a_lo = join(own_a, z1)
    ax_lo, ay_lo = across(a_lo, 1), across(a_lo, 2)
    z2 = along(z1, 1)
    b0 = join(own_b, bx, by, bd)
    z2, b0 = bar(z2, b0)
    z3 = along(z2, 1)
    weights = weights_of(dense, sum(order, []))
    ax_lo, ay_lo, z2, z3, b0, a_lo, weights = bar(ax_lo, ay_lo, z2, z3, b0, a_lo, weights)
    a_hi = join(z2, z3)
    ax_hi, ay_hi = across(a_hi, 1), across(a_hi, 2)
    b1 = along(b0, 1)
    p_axlo, p_aylo, p_b0 = call(0, [ax_lo, ay_lo, b0], [(1, BF16), (1, BF16), (1, F32)])
    ax_hi, ay_hi, b1, p_axlo, p_aylo, p_b0, ay_lo, a_lo, a_hi = bar(
        ax_hi, ay_hi, b1, p_axlo, p_aylo, p_b0, ay_lo, a_lo, a_hi
    )
    ad, ae = across(ay_lo, 1), across(ax_hi, 2)
    b2 = along(b1, 1)
    p_axhi, p_ayhi, p_b1 = call(1, [ax_hi, ay_hi, b1], [(1, BF16), (1, BF16), (1, BF16)])
    b2, p_axhi, p_ayhi, p_b1, a_lo, a_hi = bar(b2, p_axhi, p_ayhi, p_b1, a_lo, a_hi)
    b3 = along(b2, 1)
    p_a, p_b2 = call(2, [a_lo, a_hi, b2], [(2, F32), (1, BF16)])
    ad, ae, b3, p_axhi, p_ayhi, p_b1, p_a, p_b2, p_axlo, p_aylo = bar(
        ad, ae, b3, p_axhi, p_ayhi, p_b1, p_a, p_b2, p_axlo, p_aylo
    )
    got_xlo, got_ylo = across(p_axlo, 1), across(p_aylo, 2)
    got_xhi, got_yhi = across(p_axhi, 1), across(p_ayhi, 2)
    got_b1, got_b2 = along(p_b1, -1), along(p_b2, -2)
    p_d, p_b3 = call(3, [ad, ae, b3], [(2, BF16), (1, BF16)])
    got_xlo, got_ylo, got_xhi, got_yhi, got_b1, got_b2, p_d, p_b3 = bar(
        got_xlo, got_ylo, got_xhi, got_yhi, got_b1, got_b2, p_d, p_b3
    )
    got_d = across(p_d, 3)
    got_b3 = along(p_b3, -3)
    got_d, got_b3 = bar(got_d, got_b3)
    got_x, got_y = (got_xlo, got_xhi), (got_ylo, got_yhi)
    s = [
        p_a[r] + f32(got_x[r // 2][r % 2]) + f32(got_y[r // 2][r % 2]) + f32(got_d[r])
        for r in every
    ]
    got_s = [along(s[r].astype(BF16), -r) for r in (1, 2, 3)]
    s_b = p_b0 + f32(got_b1) + f32(got_b2) + f32(got_b3)
    got = [across(s_b[k].astype(BF16), k) for k in (1, 2, 3)]
    hvp_a = s[0] + f32(got_s[0]) + f32(got_s[1]) + f32(got_s[2])
    hvp_b = s_b[0] + f32(got[0]) + f32(got[1]) + f32(got[2])
    return join(hvp_a, hvp_b)


def solution(mesh):
    split = P(("dp", "expert"), None)
    return jax.shard_map(
        local,
        mesh=mesh,
        in_specs=(split,) * 5 + (P("expert", None, None),) * 3,
        out_specs=(split, P()),
        check_vma=False,
    )
```

```python
import functools

import jax
import jax.numpy as jnp
from jax import lax
from jax.experimental import pallas as pl
from jax.experimental.pallas import tpu as pltpu
from jax.sharding import PartitionSpec as P

F32, BF16 = jnp.float32, jnp.bfloat16
NT = (((1,), (1,)), ((), ()))


def expert_kernel(shapes, part, start, *refs):
    count = len(shapes)
    pieces, (gates, w_gate, w_up, w_down) = refs[:count], refs[count : count + 4]
    outs, (both, adj, total) = refs[count + 4 : -3], refs[-3:]
    rows, width = adj.shape
    experts, _, hidden = w_gate.shape
    at = 0
    for piece, (blocks, r) in zip(pieces, shapes):
        for b in range(blocks):
            both[at : at + r] = piece[b, :r]
            both[rows + at : rows + at + r] = piece[b, r : 2 * r]
            adj[at : at + r] = piece[b, 2 * r :]
            at += r

    def parts_of(e, cols):
        gate = jnp.dot(both[...], w_gate[e, :, cols], preferred_element_type=F32)
        up = jnp.dot(both[...], w_up[e, :, cols], preferred_element_type=F32)
        back = lax.dot_general(w_down[e, cols, :], adj[...], NT, preferred_element_type=F32).T
        pre, pre_dir, lin, lin_dir = gate[:rows], gate[rows:], up[:rows], up[rows:]
        s = jax.nn.sigmoid(pre)
        first = s * (1.0 + pre * (1.0 - s))
        second = s * (1.0 - s) * (2.0 + pre * (1.0 - 2.0 * s))
        part_gate = back * (lin_dir * first + lin * second * pre_dir)
        part_up = back * first * pre_dir
        return part_gate.T.astype(BF16), part_up.T.astype(BF16)

    for e in range(experts):
        parts = [parts_of(e, slice(j, j + part)) for j in range(0, hidden, part)]
        part_gate = jnp.concatenate([p[0] for p in parts], axis=0)
        part_up = jnp.concatenate([p[1] for p in parts], axis=0)
        weight = gates[e, :, start : start + rows]
        chunk = 512 if width % 512 == 0 else width
        for c in range(0, width, chunk):
            cols = slice(c, c + chunk)
            reply = jnp.dot(w_gate[e, cols, :], part_gate, preferred_element_type=F32)
            reply += jnp.dot(w_up[e, cols, :], part_up, preferred_element_type=F32)
            term = jnp.where(weight != 0.0, weight * reply.astype(BF16).astype(F32), 0.0)
            if e > 0:
                term += total[cols, :]
            if e < experts - 1:
                total[cols, :] = term
                continue
            term = term.T
            at = 0
            for out in outs:
                blocks, r, _ = out.shape
                for b in range(blocks):
                    out[b, :, cols] = term[at : at + r].astype(out.dtype)
                    at += r


def expert_call(pieces, kinds, start, gates, w_gate, w_up, w_down):
    width = pieces[0].shape[2]
    shapes = tuple((p.shape[0], p.shape[1] // 3) for p in pieces)
    rows = sum(b * r for b, r in shapes)
    experts, _, hidden = w_gate.shape
    part = 256 if hidden % 256 == 0 else hidden
    near = pl.BlockSpec(memory_space=pltpu.VMEM)
    out_shape, at = [], 0
    for number, kind in kinds:
        group = shapes[at : at + number]
        out_shape.append(
            jax.ShapeDtypeStruct((sum(b for b, _ in group), group[0][1], width), kind)
        )
        at += number
    return pl.pallas_call(
        functools.partial(expert_kernel, shapes, part, start),
        in_specs=[near] * (len(pieces) + 4),
        out_specs=[near] * len(out_shape),
        out_shape=out_shape,
        scratch_shapes=[
            pltpu.VMEM((2 * rows, width), BF16),
            pltpu.VMEM((rows, width), BF16),
            pltpu.VMEM((width, rows), F32),
        ],
        compiler_params=pltpu.CompilerParams(vmem_limit_bytes=20 * 1024 * 1024),
        cost_estimate=pl.CostEstimate(
            flops=14 * rows * width * hidden * experts,
            bytes_accessed=8 * rows * width,
            transcendentals=rows * hidden * experts,
        ),
    )(*pieces, gates, w_gate, w_up, w_down)


def pack(ranges, *arrays):
    count, width = len(arrays), arrays[0].shape[1]

    def kernel(*refs):
        sems = refs[-1]
        copies = []
        for out, (lo, hi) in zip(refs[count:-1], ranges):
            for i, ref in enumerate(refs[:count]):
                to = out.at[0, i * (hi - lo) : (i + 1) * (hi - lo)]
                copies.append(pltpu.make_async_copy(ref.at[lo:hi], to, sems.at[len(copies)]))
                copies[-1].start()
        for copy in copies:
            copy.wait()

    return pl.pallas_call(
        kernel,
        in_specs=[pl.BlockSpec(memory_space=pl.ANY)] * count,
        out_specs=[pl.BlockSpec(memory_space=pltpu.VMEM)] * len(ranges),
        out_shape=[
            jax.ShapeDtypeStruct((1, count * (hi - lo), width), arrays[0].dtype)
            for lo, hi in ranges
        ],
        scratch_shapes=[pltpu.SemaphoreType.DMA((count * len(ranges),))],
        compiler_params=pltpu.CompilerParams(vmem_limit_bytes=4 * 1024 * 1024),
    )(*arrays)


def touch(value, *mats):
    def kernel(value_ref, *refs):
        refs[-1][...] = value_ref[...]

    near = pl.BlockSpec(memory_space=pltpu.VMEM)
    return pl.pallas_call(
        kernel,
        in_specs=[near] * (1 + len(mats)),
        out_specs=near,
        out_shape=jax.ShapeDtypeStruct(value.shape, value.dtype),
        compiler_params=pltpu.CompilerParams(vmem_limit_bytes=4 * 1024 * 1024),
    )(value, *mats)


def local(tokens, tangent, adjoint, gates, expert_ids, w_gate, w_up, w_down):
    count = lax.axis_size("expert")
    me = lax.axis_index("expert")
    ring = 4
    layer = count // ring
    high, low = me // layer, me % layer
    experts = w_gate.shape[0]
    tok_rows, _ = expert_ids.shape
    mats = (w_gate, w_up, w_down)

    def across(a, k):
        return lax.ppermute(a, "expert", [(i, i ^ k) for i in range(count)])

    def along(a, r):
        return lax.ppermute(a, "expert", [(i, (i + layer * r) % count) for i in range(count)])

    all_ids = jnp.arange(experts * count, dtype=jnp.int32)
    dense = jnp.sum(
        jnp.where(expert_ids[:, :, None] == all_ids[None, None, :], gates[:, :, None], 0.0), axis=1
    )
    dense = dense.T.reshape(count, experts, tok_rows)

    def to_owners(dense):
        return lax.all_to_all(dense, "expert", split_axis=0, concat_axis=0, tiled=True)

    def weights_of(dense, listing):
        source = ((high - jnp.arange(ring)) % ring * layer)[:, None] + (low ^ jnp.arange(layer))
        dense = jnp.take(dense, source.reshape(-1), axis=0).reshape(ring, layer, experts, tok_rows)
        parts = [dense[r, k, :, slice(*rows)] for blocks, k, rows in listing for r in blocks]
        return jnp.concatenate(parts, axis=1)[:, None, :]

    if layer == 4:
        arrays = (tokens, tangent, adjoint)
        hvp = scheduled(across, along, to_owners, weights_of, dense, arrays, mats)
    else:
        rows = (0, tok_rows)
        listing = [(range(ring), k, rows) for k in range(layer)]
        weights = weights_of(to_owners(dense), listing)
        blocks = list(pack([rows], tokens, tangent, adjoint))
        for _ in range(ring - 1):
            blocks.append(along(blocks[-1], 1))
        mine = jnp.concatenate(blocks, axis=0)
        column = 0.0
        for k in range(layer):
            piece = across(mine, k) if k else mine
            (reply,) = expert_call([piece], [(1, BF16)], k * ring * tok_rows, weights, *mats)
            column += (across(reply, k) if k else reply).astype(F32)
        hvp = column[0]
        for r in range(1, ring):
            hvp += along(column[r].astype(BF16), -r).astype(F32)

    wide = tangent.astype(F32)
    sums = jnp.stack([jnp.sum(hvp * hvp), jnp.sum(wide * wide)])
    ways = lax.axis_size("dp") * count
    sums = jnp.broadcast_to(sums[None, None, :], (ways, 1, 2))
    sums = lax.all_to_all(sums, ("dp", "expert"), split_axis=0, concat_axis=0, tiled=True)
    sums = jnp.sum(sums, axis=(0, 1))
    return hvp, sums[0] / sums[1]


def scheduled(across, along, to_owners, weights_of, dense, arrays, mats):
    bar = lambda *values: lax.optimization_barrier(values)
    join = lambda *values: jnp.concatenate(values, axis=0)
    f32 = lambda value: value.astype(F32)
    tok_rows = arrays[0].shape[0]
    rows_a, rows_b = (0, 3 * tok_rows // 4), (3 * tok_rows // 4, tok_rows)
    every = (0, 1, 2, 3)

    def spread(r):
        return [((r,), k, rows_b) for k in every]

    order = [
        [((0, 1), 1, rows_a), ((0, 1), 2, rows_a)] + spread(0),
        [((2, 3), 1, rows_a), ((2, 3), 2, rows_a)] + spread(1),
        [(every, 3, rows_a)] + spread(2),
        [(every, 0, rows_a)] + spread(3),
    ]
    sizes = [sum(len(b) * (rows[1] - rows[0]) for b, _, rows in part) for part in order]

    def call(place, pieces, kinds):
        return expert_call(pieces, kinds, sum(sizes[:place]), weights, *mats)

    (own_a,) = pack([rows_a], *arrays)
    dense, *arrays = bar(dense, *arrays)
    (own_b,) = pack([rows_b], *arrays)
    z1, x0, y0 = along(own_a, 1), across(own_a, 1), across(own_a, 2)
    bx, by, bd = across(own_b, 1), across(own_b, 2), across(own_b, 3)
    taken = to_owners(dense)
    z1, own_a, own_b = bar(z1, own_a, own_b)
    z2, x1, y1 = along(z1, 1), across(z1, 1), across(z1, 2)
    z2, x0, y0, x1, y1 = bar(z2, x0, y0, x1, y1)
    z3, d0, e1 = along(z2, 1), across(y0, 1), across(x1, 2)
    weights, _ = bar(weights_of(taken, sum(order, [])), x1)
    weights = touch(weights, *mats)
    z1, z2, z3, d0, e1, x0, y0, x1, y1, bx, by, bd, own_a, own_b, weights = bar(
        z1, z2, z3, d0, e1, x0, y0, x1, y1, bx, by, bd, own_a, own_b, weights
    )
    a_hi = join(z2, z3)
    x_hi, y_hi = across(a_hi, 1), across(a_hi, 2)
    b0 = join(own_b, bx, by, bd)
    b1 = along(b0, 1)
    p_xlo, p_ylo, p_b0 = call(0, [x0, x1, y0, y1, b0], [(2, BF16), (2, BF16), (1, F32)])
    x_hi, y_hi, a_hi, b1, p_xlo, p_ylo, p_b0, own_a, z1, d0, e1 = bar(
        x_hi, y_hi, a_hi, b1, p_xlo, p_ylo, p_b0, own_a, z1, d0, e1
    )
    d2, e3 = across(y_hi[:1], 1), across(x_hi[1:], 2)
    got_xlo, got_ylo = across(p_xlo, 1), across(p_ylo, 2)
    b2 = along(b1, 1)
    p_xhi, p_yhi, p_b1 = call(1, [x_hi, y_hi, b1], [(1, BF16), (1, BF16), (1, BF16)])
    d2, e3, b2, p_xhi, p_yhi, p_b1, a_hi, own_a, z1, d0, e1 = bar(
        d2, e3, b2, p_xhi, p_yhi, p_b1, a_hi, own_a, z1, d0, e1
    )
    got_xhi, got_yhi = across(p_xhi, 1), across(p_yhi, 2)
    b3 = along(b2, 1)
    p_d, p_b2 = call(2, [d0, e1, d2, e3, b2], [(4, BF16), (1, BF16)])
    got_xlo, got_ylo, b3, p_d, p_b1, p_b2, a_hi, own_a, z1 = bar(
        got_xlo, got_ylo, b3, p_d, p_b1, p_b2, a_hi, own_a, z1
    )
    got_d = across(p_d, 3)
    got_b1, got_b2 = along(p_b1, -1), along(p_b2, -2)
    p_a, p_b3 = call(3, [own_a, z1, a_hi, b3], [(3, F32), (1, BF16)])
    got_xhi, got_yhi, got_d, got_b1, got_b2, p_a, p_b3 = bar(
        got_xhi, got_yhi, got_d, got_b1, got_b2, p_a, p_b3
    )
    got_b3 = along(p_b3, -3)
    got_x, got_y = (got_xlo, got_xhi), (got_ylo, got_yhi)
    s = [
        p_a[r] + f32(got_x[r // 2][r % 2]) + f32(got_y[r // 2][r % 2]) + f32(got_d[r])
        for r in every
    ]
    got_s = [along(s[r].astype(BF16), -r) for r in (1, 2, 3)]
    s_b = p_b0 + f32(got_b1) + f32(got_b2) + f32(got_b3)
    got = [across(s_b[k].astype(BF16), k) for k in (1, 2, 3)]
    hvp_a = s[0] + f32(got_s[0]) + f32(got_s[1]) + f32(got_s[2])
    hvp_b = s_b[0] + f32(got[0]) + f32(got[1]) + f32(got[2])
    return join(hvp_a, hvp_b)


def solution(mesh):
    split = P(("dp", "expert"), None)
    return jax.shard_map(
        local,
        mesh=mesh,
        in_specs=(split,) * 5 + (P("expert", None, None),) * 3,
        out_specs=(split, P()),
        check_vma=False,
    )
```

```python
import functools

import jax
import jax.numpy as jnp
from jax import lax
from jax.experimental import pallas as pl
from jax.experimental.pallas import tpu as pltpu
from jax.sharding import PartitionSpec as P

F32, BF16 = jnp.float32, jnp.bfloat16
NT = (((1,), (1,)), ((), ()))


def expert_kernel(shapes, part, start, *refs):
    count = len(shapes)
    pieces, (gates, w_gate, w_up, w_down) = refs[:count], refs[count : count + 4]
    outs, (both, adj, total) = refs[count + 4 : -3], refs[-3:]
    rows, width = adj.shape
    experts, _, hidden = w_gate.shape
    at = 0
    for piece, (blocks, r) in zip(pieces, shapes):
        for b in range(blocks):
            both[at : at + r] = piece[b, :r]
            both[rows + at : rows + at + r] = piece[b, r : 2 * r]
            adj[at : at + r] = piece[b, 2 * r :]
            at += r

    def parts_of(e, cols):
        gate = jnp.dot(both[...], w_gate[e, :, cols], preferred_element_type=F32)
        up = jnp.dot(both[...], w_up[e, :, cols], preferred_element_type=F32)
        back = lax.dot_general(w_down[e, cols, :], adj[...], NT, preferred_element_type=F32).T
        pre, pre_dir, lin, lin_dir = gate[:rows], gate[rows:], up[:rows], up[rows:]
        s = jax.nn.sigmoid(pre)
        first = s * (1.0 + pre * (1.0 - s))
        second = s * (1.0 - s) * (2.0 + pre * (1.0 - 2.0 * s))
        part_gate = back * (lin_dir * first + lin * second * pre_dir)
        part_up = back * first * pre_dir
        return part_gate.T.astype(BF16), part_up.T.astype(BF16)

    for e in range(experts):
        parts = [parts_of(e, slice(j, j + part)) for j in range(0, hidden, part)]
        part_gate = jnp.concatenate([p[0] for p in parts], axis=0)
        part_up = jnp.concatenate([p[1] for p in parts], axis=0)
        weight = gates[e, :, start : start + rows]
        chunk = 512 if width % 512 == 0 else width
        for c in range(0, width, chunk):
            cols = slice(c, c + chunk)
            reply = jnp.dot(w_gate[e, cols, :], part_gate, preferred_element_type=F32)
            reply += jnp.dot(w_up[e, cols, :], part_up, preferred_element_type=F32)
            term = jnp.where(weight != 0.0, weight * reply.astype(BF16).astype(F32), 0.0)
            if e > 0:
                term += total[cols, :]
            if e < experts - 1:
                total[cols, :] = term
                continue
            term = term.T
            at = 0
            for out in outs:
                blocks, r, _ = out.shape
                for b in range(blocks):
                    out[b, :, cols] = term[at : at + r].astype(out.dtype)
                    at += r


def expert_call(pieces, kinds, start, gates, w_gate, w_up, w_down):
    width = pieces[0].shape[2]
    shapes = tuple((p.shape[0], p.shape[1] // 3) for p in pieces)
    rows = sum(b * r for b, r in shapes)
    experts, _, hidden = w_gate.shape
    part = 256 if hidden % 256 == 0 else hidden
    near = pl.BlockSpec(memory_space=pltpu.VMEM)
    out_shape, at = [], 0
    for number, kind in kinds:
        group = shapes[at : at + number]
        out_shape.append(
            jax.ShapeDtypeStruct((sum(b for b, _ in group), group[0][1], width), kind)
        )
        at += number
    return pl.pallas_call(
        functools.partial(expert_kernel, shapes, part, start),
        in_specs=[near] * (len(pieces) + 4),
        out_specs=[near] * len(out_shape),
        out_shape=out_shape,
        scratch_shapes=[
            pltpu.VMEM((2 * rows, width), BF16),
            pltpu.VMEM((rows, width), BF16),
            pltpu.VMEM((width, rows), F32),
        ],
        compiler_params=pltpu.CompilerParams(vmem_limit_bytes=22 * 1024 * 1024),
        cost_estimate=pl.CostEstimate(
            flops=14 * rows * width * hidden * experts,
            bytes_accessed=8 * rows * width,
            transcendentals=rows * hidden * experts,
        ),
    )(*pieces, gates, w_gate, w_up, w_down)


def pack(ranges, *arrays):
    count, width = len(arrays), arrays[0].shape[1]

    def kernel(*refs):
        sems = refs[-1]
        copies = []
        for out, (lo, hi) in zip(refs[count:-1], ranges):
            for i, ref in enumerate(refs[:count]):
                to = out.at[0, i * (hi - lo) : (i + 1) * (hi - lo)]
                copies.append(pltpu.make_async_copy(ref.at[lo:hi], to, sems.at[len(copies)]))
                copies[-1].start()
        for copy in copies:
            copy.wait()

    return pl.pallas_call(
        kernel,
        in_specs=[pl.BlockSpec(memory_space=pl.ANY)] * count,
        out_specs=[pl.BlockSpec(memory_space=pltpu.VMEM)] * len(ranges),
        out_shape=[
            jax.ShapeDtypeStruct((1, count * (hi - lo), width), arrays[0].dtype)
            for lo, hi in ranges
        ],
        scratch_shapes=[pltpu.SemaphoreType.DMA((count * len(ranges),))],
        compiler_params=pltpu.CompilerParams(vmem_limit_bytes=4 * 1024 * 1024),
    )(*arrays)


def touch(value, *mats):
    def kernel(value_ref, *refs):
        refs[-1][...] = value_ref[...]

    near = pl.BlockSpec(memory_space=pltpu.VMEM)
    return pl.pallas_call(
        kernel,
        in_specs=[near] * (1 + len(mats)),
        out_specs=near,
        out_shape=jax.ShapeDtypeStruct(value.shape, value.dtype),
        compiler_params=pltpu.CompilerParams(vmem_limit_bytes=4 * 1024 * 1024),
    )(value, *mats)


def local(tokens, tangent, adjoint, gates, expert_ids, w_gate, w_up, w_down):
    count = lax.axis_size("expert")
    me = lax.axis_index("expert")
    ring = 4
    layer = count // ring
    high, low = me // layer, me % layer
    experts = w_gate.shape[0]
    tok_rows, _ = expert_ids.shape
    mats = (w_gate, w_up, w_down)

    def across(a, k):
        return lax.ppermute(a, "expert", [(i, i ^ k) for i in range(count)])

    def along(a, r):
        return lax.ppermute(a, "expert", [(i, (i + layer * r) % count) for i in range(count)])

    all_ids = jnp.arange(experts * count, dtype=jnp.int32)
    dense = jnp.sum(
        jnp.where(expert_ids[:, :, None] == all_ids[None, None, :], gates[:, :, None], 0.0), axis=1
    )
    dense = dense.T.reshape(count, experts, tok_rows)

    def to_owners(dense):
        return lax.all_to_all(dense, "expert", split_axis=0, concat_axis=0, tiled=True)

    def weights_of(dense, listing):
        source = ((high - jnp.arange(ring)) % ring * layer)[:, None] + (low ^ jnp.arange(layer))
        dense = jnp.take(dense, source.reshape(-1), axis=0).reshape(ring, layer, experts, tok_rows)
        parts = [dense[r, k, :, slice(*rows)] for blocks, k, rows in listing for r in blocks]
        return jnp.concatenate(parts, axis=1)[:, None, :]

    if layer == 4:
        arrays = (tokens, tangent, adjoint)
        hvp = scheduled(across, along, to_owners, weights_of, dense, arrays, mats)
    else:
        rows = (0, tok_rows)
        listing = [(range(ring), k, rows) for k in range(layer)]
        weights = weights_of(to_owners(dense), listing)
        blocks = list(pack([rows], tokens, tangent, adjoint))
        for _ in range(ring - 1):
            blocks.append(along(blocks[-1], 1))
        mine = jnp.concatenate(blocks, axis=0)
        column = 0.0
        for k in range(layer):
            piece = across(mine, k) if k else mine
            (reply,) = expert_call([piece], [(1, BF16)], k * ring * tok_rows, weights, *mats)
            column += (across(reply, k) if k else reply).astype(F32)
        hvp = column[0]
        for r in range(1, ring):
            hvp += along(column[r].astype(BF16), -r).astype(F32)

    wide = tangent.astype(F32)
    sums = jnp.stack([jnp.sum(hvp * hvp), jnp.sum(wide * wide)])
    ways = lax.axis_size("dp") * count
    sums = jnp.broadcast_to(sums[None, None, :], (ways, 1, 2))
    sums = lax.all_to_all(sums, ("dp", "expert"), split_axis=0, concat_axis=0, tiled=True)
    sums = jnp.sum(sums, axis=(0, 1))
    return hvp, sums[0] / sums[1]


def scheduled(across, along, to_owners, weights_of, dense, arrays, mats):
    bar = lambda *values: lax.optimization_barrier(values)
    join = lambda *values: jnp.concatenate(values, axis=0)
    f32 = lambda value: value.astype(F32)
    tok_rows = arrays[0].shape[0]
    rows_a, rows_b = (0, 3 * tok_rows // 4), (3 * tok_rows // 4, tok_rows)
    every = (0, 1, 2, 3)

    def spread(r):
        return [((r,), k, rows_b) for k in every]

    order = [
        [((0, 1), 1, rows_a), ((0, 1), 2, rows_a), ((0, 1), 3, rows_a)] + spread(0),
        [((2, 3), 1, rows_a), ((2, 3), 2, rows_a)] + spread(1),
        [((2, 3), 3, rows_a)] + spread(2),
        [(every, 0, rows_a)] + spread(3),
    ]
    sizes = [sum(len(b) * (rows[1] - rows[0]) for b, _, rows in part) for part in order]

    def call(place, pieces, kinds):
        return expert_call(pieces, kinds, sum(sizes[:place]), weights, *mats)

    (own_a,) = pack([rows_a], *arrays)
    dense, *arrays = bar(dense, *arrays)
    (own_b,) = pack([rows_b], *arrays)
    z1, x0, y0 = along(own_a, 1), across(own_a, 1), across(own_a, 2)
    bx, by, bd = across(own_b, 1), across(own_b, 2), across(own_b, 3)
    taken = to_owners(dense)
    z1, own_a, own_b = bar(z1, own_a, own_b)
    z2, x1, y1 = along(z1, 1), across(z1, 1), across(z1, 2)
    z2, x0, y0, x1, y1 = bar(z2, x0, y0, x1, y1)
    z3, d0, e1 = along(z2, 1), across(y0, 1), across(x1, 2)
    weights, _ = bar(weights_of(taken, sum(order, [])), x1)
    weights = touch(weights, *mats)
    z1, z2, z3, d0, e1, x0, y0, x1, y1, bx, by, bd, own_a, own_b, weights = bar(
        z1, z2, z3, d0, e1, x0, y0, x1, y1, bx, by, bd, own_a, own_b, weights
    )
    x2, y2, x3, y3 = across(z2, 1), across(z2, 2), across(z3, 1), across(z3, 2)
    b0 = join(own_b, bx, by, bd)
    b1 = along(b0, 1)
    p_xlo, p_ylo, p_d01, p_b0 = call(
        0, [x0, x1, y0, y1, d0, e1, b0], [(2, BF16), (2, BF16), (2, BF16), (1, F32)]
    )
    x2, y2, x3, y3, b1, p_xlo, p_ylo, p_d01, p_b0, own_a, z1, z2, z3 = bar(
        x2, y2, x3, y3, b1, p_xlo, p_ylo, p_d01, p_b0, own_a, z1, z2, z3
    )
    d2, e3 = across(y2, 1), across(x3, 2)
    got_xlo, got_ylo = across(p_xlo, 1), across(p_ylo, 2)
    b2 = along(b1, 1)
    p_xhi, p_yhi, p_b1 = call(1, [x2, x3, y2, y3, b1], [(2, BF16), (2, BF16), (1, BF16)])
    d2, e3, b2, p_xhi, p_yhi, p_b1, p_d01, own_a, z1, z2, z3 = bar(
        d2, e3, b2, p_xhi, p_yhi, p_b1, p_d01, own_a, z1, z2, z3
    )
    got_d01 = across(p_d01, 3)
    got_xhi, got_yhi = across(p_xhi, 1), across(p_yhi, 2)
    b3 = along(b2, 1)
    p_d23, p_b2 = call(2, [d2, e3, b2], [(2, BF16), (1, BF16)])
    got_xlo, got_ylo, b3, p_d23, p_b1, p_b2, own_a, z1, z2, z3 = bar(
        got_xlo, got_ylo, b3, p_d23, p_b1, p_b2, own_a, z1, z2, z3
    )
    got_d23 = across(p_d23, 3)
    got_b1, got_b2 = along(p_b1, -1), along(p_b2, -2)
    p_a, p_b3 = call(3, [own_a, z1, z2, z3, b3], [(4, F32), (1, BF16)])
    got_xhi, got_yhi, got_d01, got_d23, got_b1, got_b2, p_a, p_b3 = bar(
        got_xhi, got_yhi, got_d01, got_d23, got_b1, got_b2, p_a, p_b3
    )
    got_b3 = along(p_b3, -3)
    got_x, got_y, got_d = (got_xlo, got_xhi), (got_ylo, got_yhi), (got_d01, got_d23)
    s = [
        p_a[r] + f32(got_x[r // 2][r % 2]) + f32(got_y[r // 2][r % 2]) + f32(got_d[r // 2][r % 2])
        for r in every
    ]
    got_s = [along(s[r].astype(BF16), -r) for r in (1, 2, 3)]
    s_b = p_b0 + f32(got_b1) + f32(got_b2) + f32(got_b3)
    got = [across(s_b[k].astype(BF16), k) for k in (1, 2, 3)]
    hvp_a = s[0] + f32(got_s[0]) + f32(got_s[1]) + f32(got_s[2])
    hvp_b = s_b[0] + f32(got[0]) + f32(got[1]) + f32(got[2])
    return join(hvp_a, hvp_b)


def solution(mesh):
    split = P(("dp", "expert"), None)
    return jax.shard_map(
        local,
        mesh=mesh,
        in_specs=(split,) * 5 + (P("expert", None, None),) * 3,
        out_specs=(split, P()),
        check_vma=False,
    )
```
